256 devices in a mesh: grp: 4 (over x_lo, core), blk: 64 (over x_hi, z, y).
Axes of the slice: x: 4 (x_hi: 2, x_lo: 2; x = x_hi * 2 + x_lo), y: 4, z: 8, core: 2. Of those that a mesh axis runs over, the one named last changes fastest.
Arguments:
- image_feat: bfloat16 [16384, 1152], P(('grp', 'blk')), may hold values from -6 to 6
- text_feat: bfloat16 [16384, 1152], P(('grp', 'blk')), may hold values from -6 to 6
- norm_gain: float32 [1152], replicated, may hold values from 0.1 to 1.9
- w_image: bfloat16 [1152, 1152], replicated, may hold values from -1 to 1
- w_text: bfloat16 [1152, 1152], replicated, may hold values from -1 to 1
- log_scale: float32 [1], replicated, may hold values from 2 to 2.7
- bias: float32 [1], replicated, may hold values from -4 to -1
Outputs:
- d_image: bfloat16 [16384, 1152], P(('grp', 'blk'))
- d_text: bfloat16 [16384, 1152], P(('grp', 'blk'))
The draws below stay inside these ranges and needn't reach their ends.
All inputs are finite; a program needn't handle non-finite values.
Results may differ from the reference program's by a relative error of at most 0.0075.
Values may be sent and summed in bfloat16 or wider, within the bound.
No kernel may reach another device: no remote copies, remote signals or barrier semaphores. Data moves between devices by JAX's collectives and lax.ppermute only.
A program may use at most 128 MiB of HBM per device.

```python
import math
import jax
import jax.numpy as jnp
from jax import lax

D = 1152
BATCH = 16384


def shared_latent(key, own_weight):
    key = jax.random.fold_in(key, 101)
    key_own = jax.random.fold_in(key, 0)
    own_part = jax.random.normal(key_own, (BATCH, D), jnp.float32)
    return own_weight * own_part


def shared_diagonal(key):
    key = jax.random.fold_in(key, 202)
    return (2 * jax.random.randint(key, (D,), 0, 2) - 1).astype(jnp.float32)


def feature_rows(latent, key, spread):
    own_noise = jax.random.normal(key, (BATCH, D), jnp.float32)
    return jnp.clip(latent + spread * own_noise, -6.0, 6.0).astype(jnp.bfloat16)


def weight_rows(diagonal_sign, key, off_scale):
    own_part = jax.random.normal(key, (D, D), jnp.float32)
    off_part = jnp.clip(own_part, -4.0, 4.0) * off_scale * D ** (-0.5)
    row_ids = jnp.arange(D, dtype=jnp.int32)[:, None]
    col_ids = jnp.arange(D, dtype=jnp.int32)[None, :]
    values = jnp.where(row_ids == col_ids, diagonal_sign[:, None], jnp.float32(0.0)) + off_part
    return jnp.clip(values, -1.0, 1.0).astype(jnp.bfloat16)


def draw_image_feat(key, part):
    latent = shared_latent(key, 0.75)
    spread = 0.65
    key = jax.random.fold_in(key, 3)
    return feature_rows(latent, key, spread)


def draw_text_feat(key, part):
    latent = shared_latent(key, 0.75)
    spread = 0.65
    key = jax.random.fold_in(key, 4)
    return feature_rows(latent, key, spread)


def draw_w_image(key, part):
    diagonal_sign = shared_diagonal(key)
    key = jax.random.fold_in(key, 5)
    off_scale = 0.25
    return weight_rows(diagonal_sign, key, off_scale)


def draw_w_text(key, part):
    diagonal_sign = shared_diagonal(key)
    key = jax.random.fold_in(key, 6)
    off_scale = 0.25
    return weight_rows(diagonal_sign, key, off_scale)


def setup_inputs(seed: int = 0) -> dict:
    streams_of = jax.random.split(jax.random.key(seed), 8)
    image_feat = draw_image_feat(jax.random.fold_in(streams_of[7], 71), 0)
    text_feat = draw_text_feat(jax.random.fold_in(streams_of[7], 71), 0)
    norm_gain = jnp.clip(1.0 + 0.18 * jax.random.normal(streams_of[2], (D,), jnp.float32), 0.1, 1.9)
    w_image = draw_w_image(jax.random.fold_in(streams_of[7], 71), 0)
    w_text = draw_w_text(jax.random.fold_in(streams_of[7], 71), 0)
    log_scale = jnp.clip(jax.random.uniform(streams_of[5], (1,), jnp.float32, 2.0, 2.7), 2.0, 2.7)
    bias = jnp.clip(jax.random.uniform(streams_of[6], (1,), jnp.float32, -4.0, -1.0), -4.0, -1.0)
    return {"image_feat": image_feat, "text_feat": text_feat, "norm_gain": norm_gain, "w_image": w_image, "w_text": w_text, "log_scale": log_scale, "bias": bias}


def unit_rows(project):
    length = jnp.sqrt(lax.optimization_barrier(jnp.sum(project * project, axis=-1, keepdims=True)) + 1e-06)
    unit = project / length
    return (unit.astype(jnp.bfloat16), unit, length)

def image_forward(features, norm_gain, weight):
    values = features.astype(jnp.float32)
    center = values - lax.optimization_barrier(jnp.mean(values, axis=-1, keepdims=True))
    inv_std = lax.rsqrt(lax.optimization_barrier(jnp.mean(center * center, axis=-1, keepdims=True)) + 1e-06)
    normed = center * inv_std
    hidden = (normed * norm_gain).astype(jnp.bfloat16)
    project = jnp.dot(hidden, weight, preferred_element_type=jnp.float32)
    emb, unit, length = unit_rows(project)
    return (emb, unit, length, normed, inv_std)

def text_forward(features, weight):
    project = jnp.dot(features, weight, preferred_element_type=jnp.float32)
    return unit_rows(project)

def unit_backward(grad_unit, unit, length):
    return (grad_unit - unit * lax.optimization_barrier(jnp.sum(unit * grad_unit, axis=-1, keepdims=True))) / length

def image_backward(grad_unit, unit, length, normed, inv_std, norm_gain, weight):
    grad_proj = unit_backward(grad_unit, unit, length).astype(jnp.bfloat16)
    grad_hidden = jnp.dot(grad_proj, weight.T, preferred_element_type=jnp.float32)
    grad_normed = grad_hidden * norm_gain
    grad_in = inv_std * (grad_normed - lax.optimization_barrier(jnp.mean(grad_normed, axis=-1, keepdims=True)) - normed * lax.optimization_barrier(jnp.mean(grad_normed * normed, axis=-1, keepdims=True)))
    return grad_in.astype(jnp.bfloat16)

def text_backward(grad_unit, unit, length, weight):
    grad_proj = unit_backward(grad_unit, unit, length).astype(jnp.bfloat16)
    return jnp.dot(grad_proj, weight.T, preferred_element_type=jnp.float32).astype(jnp.bfloat16)

def reference(image_feat, text_feat, norm_gain, w_image, w_text, log_scale, bias):
    image_emb, image_unit, image_len, normed, inv_std = image_forward(image_feat, norm_gain, w_image)
    text_emb, text_unit, text_len = text_forward(text_feat, w_text)
    logit_scale = jnp.exp(log_scale[0])
    logit_bias = bias[0]
    block_rows = math.gcd(BATCH, 512)
    column_ids = jnp.arange(BATCH, dtype=jnp.int32)

    def one_block(text_grad, first_row):
        image_block = lax.dynamic_slice_in_dim(image_emb, first_row, block_rows, 0)
        logits = logit_scale * jnp.dot(image_block, text_emb.T, preferred_element_type=jnp.float32) + logit_bias
        row_ids = first_row + jnp.arange(block_rows, dtype=jnp.int32)
        labels = jnp.where(row_ids[:, None] == column_ids[None, :], jnp.float32(1.0), jnp.float32(-1.0))
        pair_grad = (-labels * jax.nn.sigmoid(-labels * logits)).astype(jnp.bfloat16)
        image_grad = logit_scale * jnp.dot(pair_grad, text_emb, preferred_element_type=jnp.float32)
        text_grad = text_grad + logit_scale * jnp.dot(pair_grad.T, image_block, preferred_element_type=jnp.float32)
        return (text_grad, image_grad)
    starts = jnp.arange(0, BATCH, block_rows, dtype=jnp.int32)
    text_gu, image_parts = lax.scan(one_block, jnp.zeros((BATCH, D), jnp.float32), starts)
    image_gu = image_parts.reshape(BATCH, D)
    d_image = image_backward(image_gu, image_unit, image_len, normed, inv_std, norm_gain, w_image)
    d_text = text_backward(text_gu, text_unit, text_len, w_text)
    return (d_image, d_text)
```

```python
import jax
import jax.numpy as jnp
from jax import lax
from jax.experimental import pallas as pl
from jax.experimental.pallas import tpu as pltpu
from jax.sharding import PartitionSpec as P

AXES = ("grp", "blk")
BF = jnp.bfloat16
F32 = jnp.float32
ROWS = 64
LOG2E = 1.4426950408889634


def flat(x, y, z, c):
    return ((((x % 2) * 2 + c) * 2 + x // 2) * 8 + z) * 4 + y


PLACES = [(x, y, z, c) for x in range(4) for y in range(4) for z in range(8) for c in range(2)]


def send(value, target):
    return lax.ppermute(value, AXES, [(flat(*p), flat(*target(*p))) for p in PLACES])


def send_z(value, k):
    return send(value, lambda x, y, z, c: (x, y, (z + k) % 8, c))


def send_core(value):
    return send(value, lambda x, y, z, c: (x, y, z, 1 - c))


def send_xy(value, k, second):
    def target(x, y, z, c):
        if (c == 1) == second:
            return (x, (y + k) % 4, z, c)
        return ((x + k) % 4, y, z, c)

    return send(value, target)


def unit_rows(project):
    length = jnp.sqrt(jnp.sum(project * project, axis=-1, keepdims=True) + 1e-06)
    unit = project / length
    return (unit.astype(BF), unit, length)


def image_forward(features, norm_gain, weight):
    values = features.astype(F32)
    center = values - jnp.mean(values, axis=-1, keepdims=True)
    inv_std = lax.rsqrt(jnp.mean(center * center, axis=-1, keepdims=True) + 1e-06)
    normed = center * inv_std
    hidden = (normed * norm_gain).astype(BF)
    project = jnp.dot(hidden, weight, preferred_element_type=F32)
    emb, unit, length = unit_rows(project)
    return (emb, unit, length, normed, inv_std)


def text_forward(features, weight):
    project = jnp.dot(features, weight, preferred_element_type=F32)
    return unit_rows(project)


def unit_backward(grad_unit, unit, length):
    return (grad_unit - unit * jnp.sum(unit * grad_unit, axis=-1, keepdims=True)) / length


def image_backward(grad_unit, unit, length, normed, inv_std, norm_gain, weight):
    grad_proj = unit_backward(grad_unit, unit, length).astype(BF)
    grad_hidden = jnp.dot(grad_proj, weight.T, preferred_element_type=F32)
    grad_normed = grad_hidden * norm_gain
    grad_in = inv_std * (
        grad_normed
        - jnp.mean(grad_normed, axis=-1, keepdims=True)
        - normed * jnp.mean(grad_normed * normed, axis=-1, keepdims=True)
    )
    return grad_in.astype(BF)


def text_backward(grad_unit, unit, length, weight):
    grad_proj = unit_backward(grad_unit, unit, length).astype(BF)
    return jnp.dot(grad_proj, weight.T, preferred_element_type=F32).astype(BF)


def pair_kernel(scal, i0, i1, i2, i3, t_own, t_sib, gi0, gi1, gi2, gi3, gt_own, gt_sib, img, txt, acc):
    half = t_own.shape[0]
    quarter = i0.shape[0]
    for n, ref in enumerate((i0, i1, i2, i3)):
        img[pl.ds(n * quarter, quarter), :] = ref[...]
    txt[pl.ds(0, half), :] = t_own[...]
    txt[pl.ds(half, half), :] = t_sib[...]
    slope = -scal[0] * LOG2E
    offset = -scal[1] * LOG2E
    images = img[...]
    width = 256
    for n in range(2 * half // width):
        texts = txt[pl.ds(n * width, width), :]
        cosine = lax.dot_general(images, texts, (((1,), (1,)), ((), ())), preferred_element_type=F32)
        power = cosine * slope + offset
        if n == 0:
            row = lax.broadcasted_iota(jnp.int32, power.shape, 0)
            col = lax.broadcasted_iota(jnp.int32, power.shape, 1)
            same = (row == col) & (row < ROWS)
            grad = 1.0 / (1.0 + jnp.exp2(jnp.where(same, -power, power)))
            grad = jnp.where(same, -grad, grad).astype(BF)
        else:
            grad = (1.0 / (1.0 + jnp.exp2(power))).astype(BF)
        part = jnp.dot(grad, texts, preferred_element_type=F32)
        if n == 0:
            acc[...] = part
        else:
            acc[...] += part
        back = lax.dot_general(grad, images, (((0,), (0,)), ((), ())), preferred_element_type=F32)
        if n * width < half:
            gt_own[pl.ds(n * width, width), :] = back
        else:
            gt_sib[pl.ds(n * width - half, width), :] = back.astype(BF)
    gi0[...] = acc[pl.ds(0, quarter), :]
    for n, ref in enumerate((gi1, gi2, gi3)):
        ref[...] = acc[pl.ds((n + 1) * quarter, quarter), :].astype(BF)


def pair_block(scal, images, t_own, t_sib):
    quarter, width = images[0].shape
    half = t_own.shape[0]
    shape = jax.ShapeDtypeStruct
    vmem = pl.BlockSpec(memory_space=pltpu.VMEM)
    return pl.pallas_call(
        pair_kernel,
        out_shape=[shape((quarter, width), F32)]
        + [shape((quarter, width), BF)] * 3
        + [shape((half, width), F32), shape((half, width), BF)],
        in_specs=[pl.BlockSpec(memory_space=pltpu.SMEM)] + [vmem] * 6,
        out_specs=[vmem] * 6,
        scratch_shapes=[
            pltpu.VMEM((4 * quarter, width), BF),
            pltpu.VMEM((2 * half, width), BF),
            pltpu.VMEM((4 * quarter, width), F32),
        ],
        compiler_params=pltpu.CompilerParams(vmem_limit_bytes=48 * 1024 * 1024),
        cost_estimate=pl.CostEstimate(
            flops=6 * 8 * quarter * half * width, bytes_accessed=16 * 1024 * 1024, transcendentals=0
        ),
    )(scal, *images, t_own, t_sib)


def shards(image_feat, text_feat, norm_gain, w_image, w_text, log_scale, bias):
    text_emb, text_unit, text_len = text_forward(text_feat, w_text)
    half = ROWS // 2
    fwd, bwd = [text_emb], [text_emb]
    for _ in range(3):
        fwd.append(send_z(fwd[-1], 1))
        bwd.append(send_z(bwd[-1], -1))
    far_f = send_z(fwd[3][:half], 1)
    far_b = send_z(bwd[3][half:], -1)
    text_own = jnp.concatenate(fwd + bwd[1:] + [far_f, far_b])
    text_sib = send_core(text_own)

    image_emb, image_unit, image_len, normed, inv_std = image_forward(
        image_feat, norm_gain, w_image
    )
    near = jnp.concatenate([image_emb] + [send_xy(image_emb, k, False) for k in (1, -1, 2)])
    images = [near] + [send_xy(near, k, True) for k in (1, -1, 2)]

    logit_scale = jnp.exp(log_scale)
    scal = jnp.concatenate([logit_scale, bias])
    gi0, gi1, gi2, gi3, gt_own, gt_sib = pair_block(scal, images, text_own, text_sib)

    near_sum = gi0
    for part, k in ((gi1, 1), (gi2, -1), (gi3, 2)):
        near_sum = near_sum + send_xy(part, -k, True).astype(F32)
    image_gu = near_sum[:ROWS]
    near_back = near_sum.astype(BF)
    for n, k in ((1, 1), (2, -1), (3, 2)):
        back = send_xy(near_back[n * ROWS : (n + 1) * ROWS], -k, False)
        image_gu = image_gu + back.astype(F32)

    both = gt_own + send_core(gt_sib).astype(F32)
    own, f1, f2, f3, b1, b2, b3, far = [both[n * ROWS : (n + 1) * ROWS] for n in range(8)]

    def ring(parts, far_half, k, low):
        got = send_z(far_half.astype(BF), k).astype(F32)
        if low:
            total = jnp.concatenate([parts[0][:half] + got, parts[0][half:]])
        else:
            total = jnp.concatenate([parts[0][:half], parts[0][half:] + got])
        for nxt in parts[1:]:
            total = nxt + send_z(total.astype(BF), k).astype(F32)
        return send_z(total.astype(BF), k).astype(F32)

    text_gu = own + ring((f3, f2, f1), far[:half], -1, True) + ring((b3, b2, b1), far[half:], 1, False)

    d_image = image_backward(
        logit_scale * image_gu, image_unit, image_len, normed, inv_std, norm_gain, w_image
    )
    d_text = text_backward(logit_scale * text_gu, text_unit, text_len, w_text)
    return (d_image, d_text)


def solution(mesh):
    placed = (P(AXES, None), P(AXES, None), P(), P(), P(), P(), P())
    return jax.shard_map(
        shards,
        mesh=mesh,
        in_specs=placed,
        out_specs=(P(AXES, None), P(AXES, None)),
        check_vma=False,
    )
```

```python
import functools

import jax
import jax.numpy as jnp
from jax import lax
from jax.experimental import pallas as pl
from jax.experimental.pallas import tpu as pltpu
from jax.sharding import PartitionSpec as P

AXES = ("grp", "blk")
BF = jnp.bfloat16
F32 = jnp.float32
ROWS = 64
LOG2E = 1.4426950408889634


def flat(x, y, z, c):
    return ((((x % 2) * 2 + c) * 2 + x // 2) * 8 + z) * 4 + y


PLACES = [(x, y, z, c) for x in range(4) for y in range(4) for z in range(8) for c in range(2)]


def send(value, target):
    return lax.ppermute(value, AXES, [(flat(*p), flat(*target(*p))) for p in PLACES])


def send_z(value, k):
    return send(value, lambda x, y, z, c: (x, y, (z + k) % 8, c))


def send_core(value):
    return send(value, lambda x, y, z, c: (x, y, z, 1 - c))


def send_xy(value, k, second):
    def target(x, y, z, c):
        if (c == 1) == second:
            return (x, (y + k) % 4, z, c)
        return ((x + k) % 4, y, z, c)

    return send(value, target)


def unit_rows(project):
    length = jnp.sqrt(jnp.sum(project * project, axis=-1, keepdims=True) + 1e-06)
    unit = project / length
    return (unit.astype(BF), unit, length)


def image_forward(features, norm_gain, weight):
    values = features.astype(F32)
    center = values - jnp.mean(values, axis=-1, keepdims=True)
    inv_std = lax.rsqrt(jnp.mean(center * center, axis=-1, keepdims=True) + 1e-06)
    normed = center * inv_std
    hidden = (normed * norm_gain).astype(BF)
    project = jnp.dot(hidden, weight, preferred_element_type=F32)
    emb, unit, length = unit_rows(project)
    return (emb, unit, length, normed, inv_std)


def text_forward(features, weight):
    project = jnp.dot(features, weight, preferred_element_type=F32)
    return unit_rows(project)


def unit_backward(grad_unit, unit, length):
    return (grad_unit - unit * jnp.sum(unit * grad_unit, axis=-1, keepdims=True)) / length


def image_backward(grad_unit, unit, length, normed, inv_std, norm_gain, weight):
    grad_proj = unit_backward(grad_unit, unit, length).astype(BF)
    grad_hidden = jnp.dot(grad_proj, weight.T, preferred_element_type=F32)
    grad_normed = grad_hidden * norm_gain
    grad_in = inv_std * (
        grad_normed
        - jnp.mean(grad_normed, axis=-1, keepdims=True)
        - normed * jnp.mean(grad_normed * normed, axis=-1, keepdims=True)
    )
    return grad_in.astype(BF)


def text_backward(grad_unit, unit, length, weight):
    grad_proj = unit_backward(grad_unit, unit, length).astype(BF)
    return jnp.dot(grad_proj, weight.T, preferred_element_type=F32).astype(BF)


def pair_kernel(counts, has_diag, scal, *refs):
    refs = list(refs)
    images, texts, img_old, txt_old, img_out, txt_out = [
        [refs.pop(0) for _ in range(n)] for n in counts
    ]
    img, txt, grad = refs

    def spans(group):
        at, places = 0, []
        for ref in group:
            places.append(pl.ds(at, ref.shape[0]))
            at += ref.shape[0]
        return list(zip(group, places))

    for group, whole in ((images, img), (texts, txt)):
        for ref, place in spans(group):
            whole[place, :] = ref[...]
    slope = -scal[0] * LOG2E
    offset = -scal[1] * LOG2E
    width = 256
    for n in range(txt.shape[0] // width):
        cols = pl.ds(n * width, width)
        cosine = lax.dot_general(
            img[...], txt[cols, :], (((1,), (1,)), ((), ())), preferred_element_type=F32
        )
        power = cosine * slope + offset
        if has_diag and n == 0:
            row = lax.broadcasted_iota(jnp.int32, power.shape, 0)
            col = lax.broadcasted_iota(jnp.int32, power.shape, 1)
            same = (row == col) & (row < ROWS)
            value = 1.0 / (1.0 + jnp.exp2(jnp.where(same, -power, power)))
            value = jnp.where(same, -value, value)
        else:
            value = 1.0 / (1.0 + jnp.exp2(power))
        grad[:, cols] = value.astype(BF)
    for n, (ref, place) in enumerate(spans(img_out)):
        value = jnp.dot(grad[place, :], txt[...], preferred_element_type=F32)
        if img_old:
            value = value + img_old[n][...]
        ref[...] = value.astype(ref.dtype)
    for n, (ref, place) in enumerate(spans(txt_out)):
        value = lax.dot_general(
            grad[:, place], img[...], (((0,), (0,)), ((), ())), preferred_element_type=F32
        )
        if n < len(txt_old):
            value = value + txt_old[n][...]
        ref[...] = value.astype(ref.dtype)


def pair_block(scal, images, texts, img_out, txt_out, img_old=(), txt_old=(), has_diag=False):
    width = images[0].shape[1]
    vmem = pl.BlockSpec(memory_space=pltpu.VMEM)
    m, n = sum(v.shape[0] for v in images), sum(v.shape[0] for v in texts)
    operands = [*images, *texts, *img_old, *txt_old]
    outs = [jax.ShapeDtypeStruct((r, width), d) for r, d in [*img_out, *txt_out]]
    counts = tuple(len(v) for v in (images, texts, img_old, txt_old, img_out, txt_out))
    got = pl.pallas_call(
        functools.partial(pair_kernel, counts, has_diag),
        out_shape=outs,
        in_specs=[pl.BlockSpec(memory_space=pltpu.SMEM)] + [vmem] * len(operands),
        out_specs=[vmem] * len(outs),
        scratch_shapes=[
            pltpu.VMEM((m, width), BF),
            pltpu.VMEM((n, width), BF),
            pltpu.VMEM((m, n), BF),
        ],
        compiler_params=pltpu.CompilerParams(vmem_limit_bytes=24 * 1024 * 1024),
        cost_estimate=pl.CostEstimate(flops=1024, bytes_accessed=1024, transcendentals=0),
    )(scal, *operands)
    return got[: len(img_out)], got[len(img_out) :]


def shards(image_feat, text_feat, norm_gain, w_image, w_text, log_scale, bias):
    half = ROWS // 2
    cat = jnp.concatenate
    tie = lax.optimization_barrier
    logit_scale = jnp.exp(log_scale)
    scal = cat([logit_scale, bias])

    text_emb, text_unit, text_len = text_forward(text_feat, w_text)
    f1, b1 = send_z(text_emb, 1), send_z(text_emb, -1)
    f2, b2 = send_z(f1, 1), send_z(b1, -1)
    image_emb, image_unit, image_len, normed, inv_std = image_forward(
        image_feat, norm_gain, w_image
    )
    near = [send_xy(image_emb, k, False) for k in (1, -1, 2)]
    near = cat([image_emb] + near)
    next_p, next_m = [send_xy(near, k, True) for k in (1, -1)]
    across_p = send_xy(next_p[: 2 * ROWS], 1, True)
    across_m = send_xy(next_m[2 * ROWS :], -1, True)
    far_f = send_z(cat([f1, f2[:half]]), 2)
    far_b = send_z(cat([b1, b2[half:]]), -2)
    early = cat([text_emb, f1, b1, f2])
    early_sib = send_core(early)

    sides = [near, next_p, next_m]
    side = 4 * ROWS
    side_acc, early_acc = pair_block(
        scal, sides, [early, early_sib], [(side, F32)] * 3, [(side, F32)] * 2, has_diag=True
    )
    b2, far_f, far_b, across_p, across_m, side_acc, early_acc = tie(
        (b2, far_f, far_b, across_p, across_m, side_acc, early_acc)
    )
    late = cat([b2, far_f, far_b])
    late_sib = send_core(late)
    (across_pg, across_mg), (ge_own, ge_sib, *late_acc) = pair_block(
        scal, [across_p, across_m], [early, early_sib, late, late_sib], [(2 * ROWS, BF)] * 2,
        [(side, F32), (side, BF), (side, F32), (side, F32)], txt_old=early_acc,
    )
    (near_g, next_pg, next_mg), (gl_own, gl_sib) = pair_block(
        scal, sides, [late, late_sib], [(side, F32)] * 3, [(side, F32), (side, BF)],
        img_old=side_acc, txt_old=late_acc,
    )

    across_pg, across_mg = send_xy(across_pg, -1, True), send_xy(across_mg, 1, True)
    across_pg, across_mg, gl_sib = tie((across_pg, across_mg, gl_sib))
    low, high = across_pg.astype(F32), across_mg.astype(F32)
    next_pg = cat([next_pg[: 2 * ROWS] + low, next_pg[2 * ROWS :]]).astype(BF)
    next_mg = cat([next_mg[: 2 * ROWS], next_mg[2 * ROWS :] + high]).astype(BF)
    late_sum = gl_own + send_core(gl_sib).astype(F32)
    early_sum = ge_own + send_core(ge_sib).astype(F32)

    next_pg, next_mg, late_sum, early_sum = tie((next_pg, next_mg, late_sum, early_sum))

    def hop(value, k):
        return send_z(value.astype(BF), k).astype(F32)

    near_sum = near_g
    for part, k in ((next_pg, -1), (next_mg, 1)):
        near_sum = near_sum + send_xy(part, k, True).astype(F32)
    own, s1, s2, s3 = [early_sum[n * ROWS : (n + 1) * ROWS] for n in range(4)]
    s4 = late_sum[:ROWS]
    cut = 2 * ROWS + half
    low, high = hop(late_sum[ROWS:cut], -2), hop(late_sum[cut:], 2)
    near_sum, low, high = tie((near_sum, low, high))

    near_back = near_sum.astype(BF)
    image_gu = near_sum[:ROWS]
    for n, k in ((1, 1), (2, -1), (3, 2)):
        back = send_xy(near_back[n * ROWS : (n + 1) * ROWS], -k, False)
        image_gu = image_gu + back.astype(F32)
    s1, s2 = s1 + low[:ROWS], s2 + high[:ROWS]
    s3 = cat([s3[:half] + low[ROWS:], s3[half:]])
    s4 = cat([s4[:half], s4[half:] + high[ROWS:]])
    text_gu = own + hop(s1, -1) + hop(s2, 1) + hop(s3, -2) + hop(s4, 2)

    d_image = image_backward(
        logit_scale * image_gu, image_unit, image_len, normed, inv_std, norm_gain, w_image
    )
    d_text = text_backward(logit_scale * text_gu, text_unit, text_len, w_text)
    return (d_image, d_text)


def solution(mesh):
    placed = (P(AXES, None), P(AXES, None), P(), P(), P(), P(), P())
    return jax.shard_map(
        shards,
        mesh=mesh,
        in_specs=placed,
        out_specs=(P(AXES, None), P(AXES, None)),
        check_vma=False,
    )
```

```python
import functools

import jax
import jax.numpy as jnp
from jax import lax
from jax.experimental import pallas as pl
from jax.experimental.pallas import tpu as pltpu
from jax.sharding import PartitionSpec as P

AXES = ("grp", "blk")
BF = jnp.bfloat16
F32 = jnp.float32
ROWS = 64
LOG2E = 1.4426950408889634


def flat(x, y, z, c):
    return ((((x % 2) * 2 + c) * 2 + x // 2) * 8 + z) * 4 + y


PLACES = [(x, y, z, c) for x in range(4) for y in range(4) for z in range(8) for c in range(2)]


def send(value, target):
    return lax.ppermute(value, AXES, [(flat(*p), flat(*target(*p))) for p in PLACES])


def send_z(value, k):
    return send(value, lambda x, y, z, c: (x, y, (z + k) % 8, c))


def send_ring(value, k):
    return send(value, lambda x, y, z, c: (x, y, (z + (k if c == 0 else -k)) % 8, c))


def send_core(value):
    return send(value, lambda x, y, z, c: (x, y, z, 1 - c))


def send_xy(value, k, second):
    def target(x, y, z, c):
        if (c == 1) == second:
            return (x, (y + k) % 4, z, c)
        return ((x + k) % 4, y, z, c)

    return send(value, target)


def unit_rows(project):
    length = jnp.sqrt(jnp.sum(project * project, axis=-1, keepdims=True) + 1e-06)
    unit = project / length
    return (unit.astype(BF), unit, length)


def image_forward(features, norm_gain, weight):
    values = features.astype(F32)
    center = values - jnp.mean(values, axis=-1, keepdims=True)
    inv_std = lax.rsqrt(jnp.mean(center * center, axis=-1, keepdims=True) + 1e-06)
    normed = center * inv_std
    hidden = (normed * norm_gain).astype(BF)
    project = jnp.dot(hidden, weight, preferred_element_type=F32)
    emb, unit, length = unit_rows(project)
    return (emb, unit, length, normed, inv_std)


def text_forward(features, weight):
    project = jnp.dot(features, weight, preferred_element_type=F32)
    return unit_rows(project)


def unit_backward(grad_unit, unit, length):
    return (grad_unit - unit * jnp.sum(unit * grad_unit, axis=-1, keepdims=True)) / length


def image_backward(grad_unit, unit, length, normed, inv_std, norm_gain, weight):
    grad_proj = unit_backward(grad_unit, unit, length).astype(BF)
    grad_hidden = jnp.dot(grad_proj, weight.T, preferred_element_type=F32)
    grad_normed = grad_hidden * norm_gain
    grad_in = inv_std * (
        grad_normed
        - jnp.mean(grad_normed, axis=-1, keepdims=True)
        - normed * jnp.mean(grad_normed * normed, axis=-1, keepdims=True)
    )
    return grad_in.astype(BF)


def text_backward(grad_unit, unit, length, weight):
    grad_proj = unit_backward(grad_unit, unit, length).astype(BF)
    return jnp.dot(grad_proj, weight.T, preferred_element_type=F32).astype(BF)


def pair_kernel(counts, has_diag, scal, *refs):
    refs = list(refs)
    images, texts, img_old, txt_old, img_out, txt_out = [
        [refs.pop(0) for _ in range(n)] for n in counts
    ]
    img, txt, grad = refs

    def spans(group):
        at, places = 0, []
        for ref in group:
            places.append(pl.ds(at, ref.shape[0]))
            at += ref.shape[0]
        return list(zip(group, places))

    for group, whole in ((images, img), (texts, txt)):
        for ref, place in spans(group):
            whole[place, :] = ref[...]
    slope = -scal[0] * LOG2E
    offset = -scal[1] * LOG2E
    width = 256
    for at in range(0, txt.shape[0], width):
        cols = pl.ds(at, min(width, txt.shape[0] - at))
        cosine = lax.dot_general(
            img[...], txt[cols, :], (((1,), (1,)), ((), ())), preferred_element_type=F32
        )
        power = cosine * slope + offset
        if has_diag and at == 0:
            row = lax.broadcasted_iota(jnp.int32, power.shape, 0)
            col = lax.broadcasted_iota(jnp.int32, power.shape, 1)
            same = (row == col) & (row < ROWS)
            value = 1.0 / (1.0 + jnp.exp2(jnp.where(same, -power, power)))
            value = jnp.where(same, -value, value)
        else:
            value = 1.0 / (1.0 + jnp.exp2(power))
        grad[:, cols] = value.astype(BF)
    for n, (ref, place) in enumerate(spans(img_out)):
        value = jnp.dot(grad[place, :], txt[...], preferred_element_type=F32)
        if img_old and len(img_out) == 1:
            value = value + jnp.concatenate([old[...] for old in img_old])
        elif n < len(img_old):
            value = value + img_old[n][...]
        ref[...] = value.astype(ref.dtype)
    for n, (ref, place) in enumerate(spans(txt_out)):
        value = lax.dot_general(
            grad[:, place], img[...], (((0,), (0,)), ((), ())), preferred_element_type=F32
        )
        if n < len(txt_old):
            value = value + txt_old[n][...]
        ref[...] = value.astype(ref.dtype)


def pair_block(scal, images, texts, img_out, txt_out, img_old=(), txt_old=(), has_diag=False):
    width = images[0].shape[1]
    vmem = pl.BlockSpec(memory_space=pltpu.VMEM)
    m, n = sum(v.shape[0] for v in images), sum(v.shape[0] for v in texts)
    operands = [*images, *texts, *img_old, *txt_old]
    outs = [jax.ShapeDtypeStruct((r, width), d) for r, d in [*img_out, *txt_out]]
    counts = tuple(len(v) for v in (images, texts, img_old, txt_old, img_out, txt_out))
    got = pl.pallas_call(
        functools.partial(pair_kernel, counts, has_diag),
        out_shape=outs,
        in_specs=[pl.BlockSpec(memory_space=pltpu.SMEM)] + [vmem] * len(operands),
        out_specs=[vmem] * len(outs),
        scratch_shapes=[
            pltpu.VMEM((m, width), BF),
            pltpu.VMEM((n, width), BF),
            pltpu.VMEM((m, n), BF),
        ],
        compiler_params=pltpu.CompilerParams(vmem_limit_bytes=24 * 1024 * 1024),
        cost_estimate=pl.CostEstimate(flops=1024, bytes_accessed=1024, transcendentals=0),
    )(scal, *operands)
    return got[: len(img_out)], got[len(img_out) :]


def shards(image_feat, text_feat, norm_gain, w_image, w_text, log_scale, bias):
    cat = jnp.concatenate
    tie = lax.optimization_barrier
    logit_scale = jnp.exp(log_scale)
    scal = cat([logit_scale, bias])

    text_emb, text_unit, text_len = text_forward(text_feat, w_text)
    text_emb, image_feat = tie((text_emb, image_feat))
    chip_emb = cat([text_emb, send_core(text_emb)])
    t1 = send_ring(chip_emb, 1)
    t2 = send_ring(t1, 1)
    t3 = send_ring(t2, 1)
    t4 = send_ring(t3[:ROWS], 1)
    image_emb, image_unit, image_len, normed, inv_std = image_forward(
        image_feat, norm_gain, w_image
    )
    near = cat([image_emb] + [send_xy(image_emb, k, False) for k in (1, -1, 2)])
    next_p, next_m = [send_xy(near, k, True) for k in (1, -1)]
    across_p = send_xy(next_p[: 2 * ROWS], 1, True)
    across_m = send_xy(next_m[2 * ROWS :], -1, True)
    early = cat([t1, t2])
    early = [chip_emb, early, send_core(early)]

    sides = [near, next_p, next_m]
    side = 4 * ROWS
    early_rows = [(ROWS, F32)] * 2 + [(side, F32)] * 2
    near_acc, early_acc = pair_block(
        scal, [near], early, [(side, F32)], early_rows, has_diag=True
    )
    next_acc, early_acc = pair_block(
        scal, [next_p, next_m], early, [(side, F32)] * 2, early_rows, txt_old=early_acc
    )
    side_acc = [*near_acc, *next_acc]
    t3, t4, across_p, across_m, side_acc, early_acc = tie(
        (t3, t4, across_p, across_m, side_acc, early_acc)
    )
    late = cat([t3, t4])
    late = [late, send_core(late)]
    last = 3 * ROWS
    (near_g, next_pg, next_mg, *across_acc), (gl_own, gl_sib) = pair_block(
        scal, [*sides, across_p, across_m], late,
        [(side, F32), (side, BF), (side, BF), (2 * ROWS, F32), (2 * ROWS, F32)],
        [(last, F32), (last, BF)], img_old=side_acc,
    )
    (across_g,), (g_own, g_sib, ge_own, ge_sib) = pair_block(
        scal, [across_p, across_m], early, [(side, BF)],
        [(ROWS, F32), (ROWS, BF), (side, F32), (side, BF)],
        img_old=across_acc, txt_old=early_acc,
    )

    def hop(value):
        return send_ring(value.astype(BF), -1).astype(F32)

    late_sum = gl_own + send_core(gl_sib).astype(F32)
    far = hop(late_sum[2 * ROWS :])
    next_pg, next_mg = send_xy(next_pg, -1, True), send_xy(next_mg, 1, True)
    across_g, next_pg, next_mg, _ = tie((across_g, next_pg, next_mg, far))
    across_g = send_xy(across_g, 2, True)
    near_sum = near_g + next_pg.astype(F32) + next_mg.astype(F32) + across_g.astype(F32)
    early_back = send_core(cat([g_sib, ge_sib])).astype(F32)
    far = hop(cat([late_sum[:ROWS] + far, late_sum[ROWS : 2 * ROWS]]))
    far = hop(ge_own[2 * ROWS :] + early_back[3 * ROWS :] + far)
    near_back = near_sum.astype(BF)
    image_gu = near_sum[:ROWS]
    for n, k in ((1, 1), (2, -1), (3, 2)):
        back = send_xy(near_back[n * ROWS : (n + 1) * ROWS], -k, False)
        image_gu = image_gu + back.astype(F32)
    far = hop(ge_own[: 2 * ROWS] + early_back[ROWS : 3 * ROWS] + far)
    text_gu = g_own + early_back[:ROWS] + far[:ROWS]
    text_gu = text_gu + send_core(far[ROWS:].astype(BF)).astype(F32)

    d_image = image_backward(
        logit_scale * image_gu, image_unit, image_len, normed, inv_std, norm_gain, w_image
    )
    d_text = text_backward(logit_scale * text_gu, text_unit, text_len, w_text)
    return (d_image, d_text)


def solution(mesh):
    placed = (P(AXES, None), P(AXES, None), P(), P(), P(), P(), P())
    return jax.shard_map(
        shards,
        mesh=mesh,
        in_specs=placed,
        out_specs=(P(AXES, None), P(AXES, None)),
        check_vma=False,
    )
```

```python
import functools

import jax
import jax.numpy as jnp
from jax import lax
from jax.experimental import pallas as pl
from jax.experimental.pallas import tpu as pltpu
from jax.sharding import PartitionSpec as P

AXES = ("grp", "blk")
BF = jnp.bfloat16
F32 = jnp.float32
ROWS = 64
LOG2E = 1.4426950408889634


def flat(x, y, z, c):
    return ((((x % 2) * 2 + c) * 2 + x // 2) * 8 + z) * 4 + y


PLACES = [(x, y, z, c) for x in range(4) for y in range(4) for z in range(8) for c in range(2)]


def send(value, target):
    return lax.ppermute(value, AXES, [(flat(*p), flat(*target(*p))) for p in PLACES])


def send_z(value, k):
    return send(value, lambda x, y, z, c: (x, y, (z + k) % 8, c))


def send_ring(value, k):
    return send(value, lambda x, y, z, c: (x, y, (z + (k if c == 0 else -k)) % 8, c))


def send_core(value):
    return send(value, lambda x, y, z, c: (x, y, z, 1 - c))


def send_xy(value, k, second):
    def target(x, y, z, c):
        if (c == 1) == second:
            return (x, (y + k) % 4, z, c)
        return ((x + k) % 4, y, z, c)

    return send(value, target)


def unit_rows(project):
    length = jnp.sqrt(jnp.sum(project * project, axis=-1, keepdims=True) + 1e-06)
    unit = project / length
    return (unit.astype(BF), unit, length)


def image_forward(features, norm_gain, weight):
    values = features.astype(F32)
    center = values - jnp.mean(values, axis=-1, keepdims=True)
    inv_std = lax.rsqrt(jnp.mean(center * center, axis=-1, keepdims=True) + 1e-06)
    normed = center * inv_std
    hidden = (normed * norm_gain).astype(BF)
    project = jnp.dot(hidden, weight, preferred_element_type=F32)
    emb, unit, length = unit_rows(project)
    return (emb, unit, length, normed, inv_std)


def text_forward(features, weight):
    project = jnp.dot(features, weight, preferred_element_type=F32)
    return unit_rows(project)


def unit_backward(grad_unit, unit, length):
    return (grad_unit - unit * jnp.sum(unit * grad_unit, axis=-1, keepdims=True)) / length


def image_backward(grad_unit, unit, length, normed, inv_std, norm_gain, weight):
    grad_proj = unit_backward(grad_unit, unit, length).astype(BF)
    grad_hidden = jnp.dot(grad_proj, weight.T, preferred_element_type=F32)
    grad_normed = grad_hidden * norm_gain
    grad_in = inv_std * (
        grad_normed
        - jnp.mean(grad_normed, axis=-1, keepdims=True)
        - normed * jnp.mean(grad_normed * normed, axis=-1, keepdims=True)
    )
    return grad_in.astype(BF)


def text_backward(grad_unit, unit, length, weight):
    grad_proj = unit_backward(grad_unit, unit, length).astype(BF)
    return jnp.dot(grad_proj, weight.T, preferred_element_type=F32).astype(BF)


def pair_kernel(counts, has_diag, scal, *refs):
    refs = list(refs)
    images, texts, img_old, txt_old, img_out, txt_out = [
        [refs.pop(0) for _ in range(n)] for n in counts
    ]
    img, txt, grad = refs

    def spans(group):
        at, places = 0, []
        for ref in group:
            places.append(pl.ds(at, ref.shape[0]))
            at += ref.shape[0]
        return list(zip(group, places))

    for group, whole in ((images, img), (texts, txt)):
        for ref, place in spans(group):
            whole[place, :] = ref[...]
    slope = scal[:, :1] * -LOG2E
    offset = scal[:, 1:2] * -LOG2E
    width = 256
    for at in range(0, txt.shape[0], width):
        cols = pl.ds(at, min(width, txt.shape[0] - at))
        cosine = lax.dot_general(
            img[...], txt[cols, :], (((1,), (1,)), ((), ())), preferred_element_type=F32
        )
        power = cosine * slope + offset
        if has_diag and at == 0:
            row = lax.broadcasted_iota(jnp.int32, power.shape, 0)
            col = lax.broadcasted_iota(jnp.int32, power.shape, 1)
            same = (row == col) & (row < ROWS)
            value = 1.0 / (1.0 + jnp.exp2(jnp.where(same, -power, power)))
            value = jnp.where(same, -value, value)
        else:
            value = 1.0 / (1.0 + jnp.exp2(power))
        grad[:, cols] = value.astype(BF)
    for n, (ref, place) in enumerate(spans(img_out)):
        value = jnp.dot(grad[place, :], txt[...], preferred_element_type=F32)
        if img_old and len(img_out) == 1:
            value = value + jnp.concatenate([old[...] for old in img_old])
        elif n < len(img_old):
            value = value + img_old[n][...]
        ref[...] = value.astype(ref.dtype)
    for n, (ref, place) in enumerate(spans(txt_out)):
        value = lax.dot_general(
            grad[:, place], img[...], (((0,), (0,)), ((), ())), preferred_element_type=F32
        )
        if n < len(txt_old):
            value = value + txt_old[n][...]
        ref[...] = value.astype(ref.dtype)


def pair_block(scal, images, texts, img_out, txt_out, img_old=(), txt_old=(), has_diag=False):
    width = images[0].shape[1]
    vmem = pl.BlockSpec(memory_space=pltpu.VMEM)
    m, n = sum(v.shape[0] for v in images), sum(v.shape[0] for v in texts)
    operands = [*images, *texts, *img_old, *txt_old]
    outs = [jax.ShapeDtypeStruct((r, width), d) for r, d in [*img_out, *txt_out]]
    counts = tuple(len(v) for v in (images, texts, img_old, txt_old, img_out, txt_out))
    got = pl.pallas_call(
        functools.partial(pair_kernel, counts, has_diag),
        out_shape=outs,
        in_specs=[vmem] * (1 + len(operands)),
        out_specs=[vmem] * len(outs),
        scratch_shapes=[
            pltpu.VMEM((m, width), BF),
            pltpu.VMEM((n, width), BF),
            pltpu.VMEM((m, n), BF),
        ],
        compiler_params=pltpu.CompilerParams(vmem_limit_bytes=24 * 1024 * 1024),
        cost_estimate=pl.CostEstimate(flops=1024, bytes_accessed=1024, transcendentals=0),
    )(scal, *operands)
    return got[: len(img_out)], got[len(img_out) :]


def shards(image_feat, text_feat, norm_gain, w_image, w_text, log_scale, bias):
    cat = jnp.concatenate
    tie = lax.optimization_barrier
    logit_scale = jnp.exp(log_scale)
    scal = cat([logit_scale, bias]).reshape(1, 2)

    text_emb, text_unit, text_len = text_forward(text_feat, w_text)
    text_emb, image_feat = tie((text_emb, image_feat))
    chip_emb = cat([text_emb, send_core(text_emb)])
    t1 = send_ring(chip_emb, 1)
    t2 = send_ring(t1, 1)
    t3 = send_ring(t2, 1)
    t4 = send_ring(t3[:ROWS], 1)
    image_emb, image_unit, image_len, normed, inv_std = image_forward(
        image_feat, norm_gain, w_image
    )
    near = cat([image_emb] + [send_xy(image_emb, k, False) for k in (1, -1, 2)])
    next_p, next_m = [send_xy(near, k, True) for k in (1, -1)]
    across_p = send_xy(next_p[: 2 * ROWS], 1, True)
    across_m = send_xy(next_m[2 * ROWS :], -1, True)
    early = cat([t1, t2])
    early = [chip_emb, early, send_core(early)]

    sides = [near, next_p, next_m]
    side = 4 * ROWS
    early_rows = [(ROWS, F32)] * 2 + [(side, F32)] * 2
    near_acc, early_acc = pair_block(
        scal, [near], early, [(side, F32)], early_rows, has_diag=True
    )
    next_acc, early_acc = pair_block(
        scal, [next_p, next_m], early, [(side, F32)] * 2, early_rows, txt_old=early_acc
    )
    side_acc = [*near_acc, *next_acc]
    t3, t4, across_p, across_m, side_acc, early_acc = tie(
        (t3, t4, across_p, across_m, side_acc, early_acc)
    )
    late = cat([t3, t4])
    late = [late, send_core(late)]
    last = 3 * ROWS
    (near_g, next_pg, next_mg, *across_acc), (gl_own, gl_sib) = pair_block(
        scal, [*sides, across_p, across_m], late,
        [(side, F32), (side, BF), (side, BF), (2 * ROWS, F32), (2 * ROWS, F32)],
        [(last, F32), (last, BF)], img_old=side_acc,
    )
    (across_g,), (g_own, g_sib, ge_own, ge_sib) = pair_block(
        scal, [across_p, across_m], early, [(side, BF)],
        [(ROWS, F32), (ROWS, BF), (side, F32), (side, BF)],
        img_old=across_acc, txt_old=early_acc,
    )

    def hop(value):
        return send_ring(value.astype(BF), -1).astype(F32)

    late_sum = gl_own + send_core(gl_sib).astype(F32)
    far = hop(late_sum[2 * ROWS :])
    next_pg, next_mg = send_xy(next_pg, -1, True), send_xy(next_mg, 1, True)
    across_g, next_pg, next_mg, _ = tie((across_g, next_pg, next_mg, far))
    across_g = send_xy(across_g, 2, True)
    near_sum = near_g + next_pg.astype(F32) + next_mg.astype(F32) + across_g.astype(F32)
    early_back = send_core(cat([g_sib, ge_sib])).astype(F32)
    far = hop(cat([late_sum[:ROWS] + far, late_sum[ROWS : 2 * ROWS]]))
    far = hop(ge_own[2 * ROWS :] + early_back[3 * ROWS :] + far)
    near_back = near_sum.astype(BF)
    image_gu = near_sum[:ROWS]
    for n, k in ((1, 1), (2, -1), (3, 2)):
        back = send_xy(near_back[n * ROWS : (n + 1) * ROWS], -k, False)
        image_gu = image_gu + back.astype(F32)
    far = hop(ge_own[: 2 * ROWS] + early_back[ROWS : 3 * ROWS] + far)
    text_gu = g_own + early_back[:ROWS] + far[:ROWS]
    text_gu = text_gu + send_core(far[ROWS:].astype(BF)).astype(F32)

    d_image = image_backward(
        logit_scale * image_gu, image_unit, image_len, normed, inv_std, norm_gain, w_image
    )
    d_text = text_backward(logit_scale * text_gu, text_unit, text_len, w_text)
    return (d_image, d_text)


def solution(mesh):
    placed = (P(AXES, None), P(AXES, None), P(), P(), P(), P(), P())
    return jax.shard_map(
        shards,
        mesh=mesh,
        in_specs=placed,
        out_specs=(P(AXES, None), P(AXES, None)),
        check_vma=False,
    )
```

```python
import functools

import jax
import jax.numpy as jnp
from jax import lax
from jax.experimental import pallas as pl
from jax.experimental.pallas import tpu as pltpu
from jax.sharding import PartitionSpec as P

AXES = ("grp", "blk")
BF = jnp.bfloat16
F32 = jnp.float32
ROWS = 64
LOG2E = 1.4426950408889634


def flat(x, y, z, c):
    return ((((x % 2) * 2 + c) * 2 + x // 2) * 8 + z) * 4 + y


PLACES = [(x, y, z, c) for x in range(4) for y in range(4) for z in range(8) for c in range(2)]


def send(value, target):
    return lax.ppermute(value, AXES, [(flat(*p), flat(*target(*p))) for p in PLACES])


def send_z(value, k):
    return send(value, lambda x, y, z, c: (x, y, (z + k) % 8, c))


def send_ring(value, k):
    return send(value, lambda x, y, z, c: (x, y, (z + (k if c == 0 else -k)) % 8, c))


def send_core(value):
    return send(value, lambda x, y, z, c: (x, y, z, 1 - c))


def send_xy(value, k, second):
    def target(x, y, z, c):
        if (c == 1) == second:
            return (x, (y + k) % 4, z, c)
        return ((x + k) % 4, y, z, c)

    return send(value, target)


def unit_rows(project):
    length = jnp.sqrt(jnp.sum(project * project, axis=-1, keepdims=True) + 1e-06)
    unit = project / length
    return (unit.astype(BF), unit, length)


def image_forward(features, norm_gain, weight):
    values = features.astype(F32)
    center = values - jnp.mean(values, axis=-1, keepdims=True)
    inv_std = lax.rsqrt(jnp.mean(center * center, axis=-1, keepdims=True) + 1e-06)
    normed = center * inv_std
    hidden = (normed * norm_gain).astype(BF)
    project = jnp.dot(hidden, weight, preferred_element_type=F32)
    emb, unit, length = unit_rows(project)
    return (emb, unit, length, normed, inv_std)


def text_forward(features, weight):
    project = jnp.dot(features, weight, preferred_element_type=F32)
    return unit_rows(project)


def unit_backward(grad_unit, unit, length):
    return (grad_unit - unit * jnp.sum(unit * grad_unit, axis=-1, keepdims=True)) / length


def image_backward(grad_unit, unit, length, normed, inv_std, norm_gain, weight):
    grad_proj = unit_backward(grad_unit, unit, length).astype(BF)
    grad_hidden = jnp.dot(grad_proj, weight.T, preferred_element_type=F32)
    grad_normed = grad_hidden * norm_gain
    grad_in = inv_std * (
        grad_normed
        - jnp.mean(grad_normed, axis=-1, keepdims=True)
        - normed * jnp.mean(grad_normed * normed, axis=-1, keepdims=True)
    )
    return grad_in.astype(BF)


def text_backward(grad_unit, unit, length, weight):
    grad_proj = unit_backward(grad_unit, unit, length).astype(BF)
    return jnp.dot(grad_proj, weight.T, preferred_element_type=F32).astype(BF)


def pair_kernel(counts, has_diag, scal, *refs):
    refs = list(refs)
    images, texts, img_old, txt_old, img_out, txt_out = [
        [refs.pop(0) for _ in range(n)] for n in counts
    ]
    img, txt, grad = refs

    def spans(group):
        at, places = 0, []
        for ref in group:
            places.append(pl.ds(at, ref.shape[0]))
            at += ref.shape[0]
        return list(zip(group, places))

    for group, whole in ((images, img), (texts, txt)):
        for ref, place in spans(group):
            whole[place, :] = ref[...]
    slope = scal[:, :1] * -LOG2E
    offset = scal[:, 1:2] * -LOG2E
    width = 256
    starts = list(range(0, txt.shape[0], width))

    def chunk(at):
        return pl.ds(at, min(width, txt.shape[0] - at))

    def cosines(at):
        return lax.dot_general(
            img[...], txt[chunk(at), :], (((1,), (1,)), ((), ())), preferred_element_type=F32
        )

    following = cosines(0)
    for at in starts:
        power = following * slope + offset
        if at + width < txt.shape[0]:
            following = cosines(at + width)
        if has_diag and at == 0:
            row = lax.broadcasted_iota(jnp.int32, power.shape, 0)
            col = lax.broadcasted_iota(jnp.int32, power.shape, 1)
            same = (row == col) & (row < ROWS)
            value = 1.0 / (1.0 + jnp.exp2(jnp.where(same, -power, power)))
            value = jnp.where(same, -value, value)
        else:
            value = 1.0 / (1.0 + jnp.exp2(power))
        grad[:, chunk(at)] = value.astype(BF)
    for n, (ref, place) in enumerate(spans(img_out)):
        value = jnp.dot(grad[place, :], txt[...], preferred_element_type=F32)
        if img_old and len(img_out) == 1:
            value = value + jnp.concatenate([old[...] for old in img_old])
        elif n < len(img_old):
            value = value + img_old[n][...]
        ref[...] = value.astype(ref.dtype)
    for n, (ref, place) in enumerate(spans(txt_out)):
        value = lax.dot_general(
            grad[:, place], img[...], (((0,), (0,)), ((), ())), preferred_element_type=F32
        )
        if n < len(txt_old):
            value = value + txt_old[n][...]
        ref[...] = value.astype(ref.dtype)


def pair_block(scal, images, texts, img_out, txt_out, img_old=(), txt_old=(), has_diag=False):
    width = images[0].shape[1]
    vmem = pl.BlockSpec(memory_space=pltpu.VMEM)
    m, n = sum(v.shape[0] for v in images), sum(v.shape[0] for v in texts)
    operands = [*images, *texts, *img_old, *txt_old]
    outs = [jax.ShapeDtypeStruct((r, width), d) for r, d in [*img_out, *txt_out]]
    counts = tuple(len(v) for v in (images, texts, img_old, txt_old, img_out, txt_out))
    got = pl.pallas_call(
        functools.partial(pair_kernel, counts, has_diag),
        out_shape=outs,
        in_specs=[vmem] * (1 + len(operands)),
        out_specs=[vmem] * len(outs),
        scratch_shapes=[
            pltpu.VMEM((m, width), BF),
            pltpu.VMEM((n, width), BF),
            pltpu.VMEM((m, n), BF),
        ],
        compiler_params=pltpu.CompilerParams(vmem_limit_bytes=24 * 1024 * 1024),
        cost_estimate=pl.CostEstimate(flops=1024, bytes_accessed=1024, transcendentals=0),
    )(scal, *operands)
    return got[: len(img_out)], got[len(img_out) :]


def shards(image_feat, text_feat, norm_gain, w_image, w_text, log_scale, bias):
    cat = jnp.concatenate
    tie = lax.optimization_barrier
    logit_scale = jnp.exp(log_scale)
    scal = cat([logit_scale, bias]).reshape(1, 2)

    text_emb, text_unit, text_len = text_forward(text_feat, w_text)
    text_emb, image_feat = tie((text_emb, image_feat))
    chip_emb = cat([text_emb, send_core(text_emb)])
    t1 = send_ring(chip_emb, 1)
    t2 = send_ring(t1, 1)
    t3 = send_ring(t2, 1)
    t4 = send_ring(t3[:ROWS], 1)
    image_emb, image_unit, image_len, normed, inv_std = image_forward(
        image_feat, norm_gain, w_image
    )
    near = cat([image_emb] + [send_xy(image_emb, k, False) for k in (1, -1, 2)])
    next_p, next_m = [send_xy(near, k, True) for k in (1, -1)]
    across_p = send_xy(next_p[: 2 * ROWS], 1, True)
    across_m = send_xy(next_m[2 * ROWS :], -1, True)
    early = cat([t1, t2])
    early = [chip_emb, early, send_core(early)]

    sides = [near, next_p, next_m]
    side = 4 * ROWS
    early_rows = [(ROWS, F32)] * 2 + [(side, F32)] * 2
    near_acc, early_acc = pair_block(
        scal, [near], early, [(side, F32)], early_rows, has_diag=True
    )
    next_acc, early_acc = pair_block(
        scal, [next_p, next_m], early, [(side, F32)] * 2, early_rows, txt_old=early_acc
    )
    side_acc = [*near_acc, *next_acc]
    t3, t4, across_p, across_m, side_acc, early_acc = tie(
        (t3, t4, across_p, across_m, side_acc, early_acc)
    )
    late = cat([t3, t4])
    late = [late, send_core(late)]
    last = 3 * ROWS
    (near_g, next_pg, next_mg, *across_acc), (gl_own, gl_sib) = pair_block(
        scal, [*sides, across_p, across_m], late,
        [(side, F32), (side, BF), (side, BF), (2 * ROWS, F32), (2 * ROWS, F32)],
        [(last, F32), (last, BF)], img_old=side_acc,
    )
    (across_g,), (g_own, g_sib, ge_own, ge_sib) = pair_block(
        scal, [across_p, across_m], early, [(side, BF)],
        [(ROWS, F32), (ROWS, BF), (side, F32), (side, BF)],
        img_old=across_acc, txt_old=early_acc,
    )

    def hop(value):
        return send_ring(value.astype(BF), -1).astype(F32)

    late_sum = gl_own + send_core(gl_sib).astype(F32)
    far = hop(late_sum[2 * ROWS :])
    next_pg, next_mg = send_xy(next_pg, -1, True), send_xy(next_mg, 1, True)
    across_g, next_pg, next_mg, _ = tie((across_g, next_pg, next_mg, far))
    across_g = send_xy(across_g, 2, True)
    near_sum = near_g + next_pg.astype(F32) + next_mg.astype(F32) + across_g.astype(F32)
    early_back = send_core(cat([g_sib, ge_sib])).astype(F32)
    far = hop(cat([late_sum[:ROWS] + far, late_sum[ROWS : 2 * ROWS]]))
    far = hop(ge_own[2 * ROWS :] + early_back[3 * ROWS :] + far)
    near_back = near_sum.astype(BF)
    image_gu = near_sum[:ROWS]
    for n, k in ((1, 1), (2, -1), (3, 2)):
        back = send_xy(near_back[n * ROWS : (n + 1) * ROWS], -k, False)
        image_gu = image_gu + back.astype(F32)
    far = hop(ge_own[: 2 * ROWS] + early_back[ROWS : 3 * ROWS] + far)
    text_gu = g_own + early_back[:ROWS] + far[:ROWS]
    text_gu = text_gu + send_core(far[ROWS:].astype(BF)).astype(F32)

    d_image = image_backward(
        logit_scale * image_gu, image_unit, image_len, normed, inv_std, norm_gain, w_image
    )
    d_text = text_backward(logit_scale * text_gu, text_unit, text_len, w_text)
    return (d_image, d_text)


def solution(mesh):
    placed = (P(AXES, None), P(AXES, None), P(), P(), P(), P(), P())
    return jax.shard_map(
        shards,
        mesh=mesh,
        in_specs=placed,
        out_specs=(P(AXES, None), P(AXES, None)),
        check_vma=False,
    )
```
